32 devices in a mesh: wide: 8 (over y, x, core), rep: 4 (over z).
Axes of the slice: x: 2, y: 2, z: 4, core: 2. Of those that a mesh axis runs over, the one named last changes fastest.
Arguments:
- record: bfloat16 [32, 256, 8192], P(('wide', 'rep')), may hold values from -90 to 90
- valid: int32 [32, 8192], P(('wide', 'rep')), may hold values 0 or 1
- sources: int32 [3], replicated, may hold values from 0 to 127
Outputs:
- stacks: float32 [128, 192, 8192], P('rep', None, 'wide')
The draws below stay inside these ranges and needn't reach their ends.
Inputs may be any that keep to these rules, and one draw needn't show every extreme that they name: `sources`: block b holds the channels 64 * b to 64 * b + 63.
All inputs are finite; a program needn't handle non-finite values. No bound on the sum of `valid` on one device may be relied on, other than what follows from the above.
Results may differ from the reference program's by a relative error of at most 0.0014.
Values may be sent and summed in bfloat16 or wider, within the bound.
A program may use at most 320 MiB of HBM per device.

```python
import math
import jax
import jax.numpy as jnp
from jax import lax

CH = 8192
WLEN = 256
SRC = 64
NBLK = 3
NSRC = 192
LAGS = 128
HALF_SMOOTH = 5
WINDOWS = 32


def draw_record(key, part):
    keys = jax.random.split(key, 6)
    shape = (WINDOWS, WLEN, CH)
    base = jnp.clip(jax.random.normal(keys[0], shape, jnp.float32), -4.0, 4.0)
    channel_scale = jnp.exp(jax.random.uniform(keys[1], (1, 1, CH), jnp.float32, 0.0, math.log(10.0)))
    window_scale = jax.random.uniform(keys[2], (WINDOWS, 1, CH), jnp.float32, 0.5, 2.0)
    frequency = jax.random.uniform(keys[3], (), jnp.float32, 0.03, 0.2)
    window_phase = jax.random.uniform(keys[4], (WINDOWS, 1, 1), jnp.float32, -math.pi, math.pi)
    channel_phase = jax.random.uniform(keys[5], (1, 1, CH), jnp.float32, -0.5, 0.5)
    times = jnp.arange(WLEN, dtype=jnp.int32).astype(jnp.float32)[None, :, None]
    tone = 0.5 * jnp.sin(2.0 * math.pi * frequency * times + window_phase + channel_phase)
    return ((base + tone) * window_scale * channel_scale).astype(jnp.bfloat16)


def plant(entries, own_key, low, high):
    index_at = [jax.random.randint(jax.random.fold_in(own_key, axis), (), 0, length) for axis, length in enumerate(entries.shape)]
    widest = entries.shape.index(max(entries.shape))
    beside = index_at[:widest] + [(index_at[widest] + 1) % entries.shape[widest]] + index_at[widest + 1:]
    return entries.at[tuple(index_at)].set(low).at[tuple(beside)].set(high)


def setup_inputs(seed: int = 0) -> dict:
    seeds = jax.random.split(jax.random.key(seed), 4)
    return {
        "record": draw_record(jax.random.fold_in(seeds[3], 71), 0),
        "valid": plant((jax.random.randint(seeds[1], (WINDOWS, CH), 0, 8) < 7).astype(jnp.int32), jax.random.fold_in(seeds[1], 1), 0, 1),
        "sources": jax.random.randint(seeds[2], (NBLK,), 0, CH // SRC).astype(jnp.int32),
    }


EPSILON = 1e-05
LEVEL_SHARE = 0.2

def hann_window(length):
    times = jnp.arange(length, dtype=jnp.int32).astype(jnp.float32)
    return 0.5 - 0.5 * jnp.cos(2.0 * math.pi / length * times)

def forward_table(length, bins):
    times = jnp.arange(length, dtype=jnp.int32)[:, None]
    freqs = jnp.arange(1, bins + 1, dtype=jnp.int32)[None, :]
    phase = 2.0 * math.pi / length * jnp.mod(times * freqs, length).astype(jnp.float32)
    return jnp.concatenate([jnp.cos(phase), -jnp.sin(phase)], axis=1).astype(jnp.bfloat16)

def inverse_table(length, bins, lags):
    freqs = jnp.arange(1, bins + 1, dtype=jnp.int32)[:, None]
    shifts = jnp.arange(lags, dtype=jnp.int32)[None, :] - lags // 2
    phase = 2.0 * math.pi / length * jnp.mod(freqs * shifts, length).astype(jnp.float32)
    return jnp.stack([jnp.cos(phase), -jnp.sin(phase)])

def band_matrix(bins):
    rows = jnp.arange(bins, dtype=jnp.int32)[:, None]
    cols = jnp.arange(bins, dtype=jnp.int32)[None, :]
    near = (jnp.abs(rows - cols) <= HALF_SMOOTH).astype(jnp.float32)
    return near / lax.optimization_barrier(jnp.sum(near, axis=1, keepdims=True))

def transform(samples, flags):
    length = samples.shape[1]
    bins = length // 2
    wide_data = samples.astype(jnp.float32)
    centered = wide_data - lax.optimization_barrier(jnp.mean(wide_data, axis=1, keepdims=True))
    tapered = (centered * hann_window(length)[None, :, None]).astype(jnp.bfloat16)
    spectrum = jnp.einsum('wtc,tg->wgc', tapered.astype(jnp.float32), forward_table(length, bins).astype(jnp.float32), precision=lax.Precision.HIGHEST)
    spectrum = spectrum.reshape(spectrum.shape[0], 2, bins, spectrum.shape[2])
    magnitude = jnp.sqrt(spectrum[:, 0] * spectrum[:, 0] + spectrum[:, 1] * spectrum[:, 1])
    smooth = jnp.einsum('fg,wgc->wfc', band_matrix(bins), magnitude, precision=lax.Precision.HIGHEST)
    level = lax.optimization_barrier(jnp.mean(magnitude, axis=1, keepdims=True))
    scaled = spectrum / (smooth + LEVEL_SHARE * level + EPSILON)[:, None]
    scaled = scaled * flags.astype(jnp.float32)[:, None, None, :]
    return scaled.astype(jnp.bfloat16)

def cross_terms(source, receiver):
    source_f = source.astype(jnp.float32)
    receiver_f = receiver.astype(jnp.float32)
    high = lax.Precision.HIGHEST
    real_real = jnp.einsum('wfs,wfc->fsc', source_f[:, 0], receiver_f[:, 0], precision=high)
    imag_imag = jnp.einsum('wfs,wfc->fsc', source_f[:, 1], receiver_f[:, 1], precision=high)
    real_imag = jnp.einsum('wfs,wfc->fsc', source_f[:, 0], receiver_f[:, 1], precision=high)
    imag_real = jnp.einsum('wfs,wfc->fsc', source_f[:, 1], receiver_f[:, 0], precision=high)
    return jnp.stack([real_real + imag_imag, real_imag - imag_real])

def reference(record, valid, sources):
    windows, length, channels = record.shape
    bins = length // 2
    picked = jnp.concatenate([lax.dynamic_slice_in_dim(record, sources[number] * SRC, SRC, 2) for number in range(NBLK)], axis=2)
    picked_flags = jnp.concatenate([lax.dynamic_slice_in_dim(valid, sources[number] * SRC, SRC, 1) for number in range(NBLK)], axis=1)
    source = transform(picked, picked_flags)
    block = math.gcd(channels, 128)
    table = inverse_table(length, bins, LAGS) * (1.0 / math.sqrt(windows * bins))

    def one_block(number):
        start = (number * block).astype(jnp.int32)
        samples = lax.dynamic_slice_in_dim(record, start, block, 2)
        flags = lax.dynamic_slice_in_dim(valid, start, block, 1)
        receiver = transform(samples, flags)
        cross = cross_terms(source, receiver)
        return jnp.einsum('kfl,kfsc->lsc', table, cross, precision=lax.Precision.HIGHEST)
    stacked = lax.map(one_block, jnp.arange(channels // block, dtype=jnp.int32))
    return jnp.transpose(stacked, (1, 2, 0, 3)).reshape(LAGS, NSRC, channels)
```

```python
import functools
import math

import jax
import jax.numpy as jnp
import numpy as np
from jax import lax
from jax.experimental import pallas as pl
from jax.experimental.pallas import tpu as pltpu
from jax.sharding import PartitionSpec as P

SRC = 64
LAGS = 128
HALF_SMOOTH = 5
EPSILON = 1e-05
LEVEL_SHARE = 0.2

VMEM_LIMIT = 56 * 1024 * 1024
TILE_LAGS = 4
LAST_TILE_LAGS = 2
PAIR = 2
RAISE = 2.0**16
MESH = pl.DeviceIdType.MESH


def forward_table(length, bins):
    phase = 2.0 * math.pi / length * np.mod(np.outer(np.arange(1, bins + 1), np.arange(length)), length)
    return jnp.asarray(np.concatenate([np.cos(phase), -np.sin(phase)], axis=0), jnp.bfloat16)


def hann_window(length):
    return jnp.asarray(0.5 - 0.5 * np.cos(2.0 * math.pi / length * np.arange(length)), jnp.float32)[:, None]


def band_matrix(bins):
    rows = np.arange(bins)
    near = (np.abs(rows[:, None] - rows[None, :]) <= HALF_SMOOTH).astype(np.float32)
    return jnp.asarray(near, jnp.bfloat16), jnp.asarray(1.0 / near.sum(axis=1, keepdims=True), jnp.float32)


def rotation_tables(length, bins):
    shifts = np.arange(LAGS) - LAGS // 2
    phase = 2.0 * math.pi / length * np.mod(np.outer(shifts, np.arange(1, bins + 1)), length)
    return jnp.asarray(np.stack([np.cos(phase), np.sin(phase)], 1) * RAISE, jnp.float32)


def whiten_tile(samples, flags, table, taper, band, inverse_count):
    bins = band.shape[0]
    samples = samples.astype(jnp.float32)
    centered = samples - jnp.mean(samples, axis=0, keepdims=True)
    tapered = (centered * taper).astype(jnp.bfloat16)
    spectrum = jnp.dot(table, tapered, preferred_element_type=jnp.float32)
    real, imag = spectrum[:bins], spectrum[bins:]
    magnitude = jnp.sqrt(real * real + imag * imag)
    smooth = jnp.zeros_like(magnitude)
    rest = magnitude
    for _ in range(3):
        piece = rest.astype(jnp.bfloat16)
        rest = rest - piece.astype(jnp.float32)
        smooth = smooth + jnp.dot(band, piece, preferred_element_type=jnp.float32)
    smooth = smooth * inverse_count
    level = jnp.mean(magnitude, axis=0, keepdims=True)
    gain = flags.astype(jnp.float32) / (smooth + (LEVEL_SHARE * level + EPSILON))
    return real * gain, imag * gain


def rotate_split(source, rotation_ref, first_lag, lags, high_ref, low_ref):
    for window in range(len(source)):
        spectrum = source[window].astype(jnp.float32)
        rows, depth = spectrum.shape
        half = depth // 2
        real, imag = spectrum[:, :half], spectrum[:, half:]
        for lag in range(lags):
            cos, sin = rotation_ref[first_lag + lag, 0:1], rotation_ref[first_lag + lag, 1:2]
            for part, value in enumerate((real * cos + imag * sin, imag * cos - real * sin)):
                high = value.astype(jnp.bfloat16)
                column = window * depth + part * half
                at = (slice(lag * rows, (lag + 1) * rows), slice(column, column + half))
                high_ref[at] = high
                low_ref[at] = (value - high.astype(jnp.float32)).astype(low_ref.dtype)


def gather_kernel(
    wide_count,
    rep_count,
    record_ref,
    valid_ref,
    picked_ref,
    picked_valid_ref,
    table_ref,
    taper_ref,
    band_ref,
    inverse_count_ref,
    rotation_ref,
    stacks_ref,
    last_receiver_ref,
    last_source_ref,
    spectra,
    sources,
    total,
    coarse,
    high_a,
    low_a,
    high_b,
    low_b,
    raw_sem,
    out_sem,
    send_sem,
    recv_sem,
    source_send_sem,
    source_recv_sem,
    share_sem,
):
    wide, rep = lax.axis_index("wide"), lax.axis_index("rep")
    slots = wide_count * rep_count
    forwarded = slots - wide_count
    length, shard = table_ref.shape[1], total.shape[1]
    rows = picked_ref.shape[1]
    bits = wide_count.bit_length() - 1
    following = (wide, lax.rem(rep + 1, rep_count))
    preceding = (wide, lax.rem(rep + rep_count - 1, rep_count))

    def peer(step):
        index = 0
        for bit in range(bits):
            index = index + ((wide // 2**bit + step // 2**bit) % 2) * 2**bit
        return index

    def slot_rows(slot):
        return pl.ds(pl.multiple_of(slot * length, length), length)

    def spectra_copy(source, target, device, sem):
        return pltpu.make_async_remote_copy(
            src_ref=spectra.at[slot_rows(source)],
            dst_ref=spectra.at[slot_rows(target)],
            send_sem=send_sem.at[sem],
            recv_sem=recv_sem.at[target],
            device_id=device,
            device_id_type=MESH,
        )

    def onward(slot):
        return spectra_copy(slot, slot + wide_count, following, slot)

    def exchange(step):
        return spectra_copy(slots - 1 + step, step, (peer(step), rep), forwarded + step)

    def source_copy(source, target, device, sem):
        return pltpu.make_async_remote_copy(
            src_ref=sources.at[source],
            dst_ref=sources.at[target],
            send_sem=sem,
            recv_sem=source_recv_sem.at[target],
            device_id=device,
            device_id_type=MESH,
        )

    def source_onward(step):
        return source_copy(step * wide_count, (step + 1) * wide_count, following, source_send_sem.at[step])

    def source_share(step, number):
        slot = step * wide_count
        return source_copy(slot, slot + number, (peer(number), rep), share_sem.at[slot + number])

    def raw_copy(step, slot):
        columns = pl.ds(pl.multiple_of(peer(step) * shard, shard), shard)
        return pltpu.make_async_copy(record_ref.at[:, columns], spectra.at[slot_rows(slot)], raw_sem.at[step])

    def wait_slot(slot):
        spectra_copy(slot, slot, following, slot).wait_recv()

    def wait_source(slot):
        source_copy(slot, slot, following, share_sem.at[slot]).wait_recv()

    def ready(slot):
        wait_slot(slot)

        @pl.when(slot < forwarded)
        def _():
            onward(slot).start()

    def share_sources(step):
        if step:
            wait_source(step * wide_count)
        if step < rep_count - 1:
            source_onward(step).start()

        @pl.loop(1, wide_count)
        def _(number):
            source_share(step, number).start()

    def whiten(step, slot):
        tile = min(512, shard)
        bins = length // 2

        @pl.loop(0, shard // tile)
        def _(number):
            columns = pl.ds(pl.multiple_of(number * tile, tile), tile)
            start = pl.multiple_of(peer(step) * shard + number * tile, tile)
            real, imag = whiten_tile(
                spectra[slot_rows(slot), columns],
                valid_ref[:, pl.ds(start, tile)],
                table_ref[...],
                taper_ref[...],
                band_ref[...],
                inverse_count_ref[...],
            )
            at = pl.multiple_of(slot * length, length)
            spectra[pl.ds(at, bins), columns] = real.astype(jnp.bfloat16)
            spectra[pl.ds(at + bins, bins), columns] = imag.astype(jnp.bfloat16)

    barrier = pltpu.get_barrier_semaphore()
    pl.semaphore_signal(barrier, inc=1, device_id=preceding, device_id_type=MESH)

    @pl.loop(1, wide_count)
    def _(step):
        pl.semaphore_signal(barrier, inc=1, device_id=(peer(step), rep), device_id_type=MESH)

    raw_copy(0, 0).start()

    @pl.loop(1, wide_count)
    def _(step):
        raw_copy(step, slots - 1 + step).start()

    real, imag = whiten_tile(
        picked_ref[...],
        picked_valid_ref[...],
        table_ref[...],
        taper_ref[...],
        band_ref[...],
        inverse_count_ref[...],
    )
    sources[0] = jnp.concatenate([real, imag], axis=0).T.astype(jnp.bfloat16)
    pl.semaphore_wait(barrier, wide_count)
    share_sources(0)
    raw_copy(0, 0).wait()
    whiten(0, 0)
    onward(0).start()

    @pl.loop(1, wide_count)
    def _(step):
        raw_copy(step, slots - 1 + step).wait()
        whiten(step, slots - 1 + step)
        exchange(step).start()

        @pl.when(step == 3)
        def _():
            ready(1)
            share_sources(1)

    total[...] = jnp.zeros_like(total)

    lags = LAGS // rep_count
    tiles = lags // TILE_LAGS
    tile_rows = TILE_LAGS * rows
    tile = min(256, shard)

    def add(pair, number, high_ref, low_ref):
        at = pl.ds(pl.multiple_of(number * tile_rows, tile_rows), tile_rows)
        depth = pl.ds(pl.multiple_of(pair * PAIR * length, PAIR * length), PAIR * length)
        for first in range(0, shard, tile):
            columns = slice(first, first + tile)
            value = jnp.dot(high_ref[...], spectra[depth, columns], preferred_element_type=jnp.float32)
            value = value + jnp.dot(low_ref[...], coarse[:, columns], preferred_element_type=jnp.float32)
            total[at, columns] += value

    @pl.loop(0, slots // PAIR - 1)
    def _(pair):
        first = pair * PAIR

        @pl.when(first < wide_count - PAIR)
        def _():
            ready(first + 2)

        @pl.when(first >= wide_count)
        def _():
            ready(first)
            ready(first + 1)

        @pl.when(first % wide_count != 0)
        def _():
            wait_source(first)

        wait_source(first + 1)
        for step in range(2, rep_count):

            @pl.when(pair == step - 2)
            def _():
                share_sources(step)

        coarse[...] = spectra[pl.ds(pl.multiple_of(first * length, PAIR * length), PAIR * length), :].astype(coarse.dtype)
        source = [sources.at[first + number] for number in range(PAIR)]

        def rotate(number, high_ref, low_ref):
            rotate_split([ref[...] for ref in source], rotation_ref, rep * lags + number * TILE_LAGS, TILE_LAGS, high_ref, low_ref)

        rotate(0, high_a, low_a)

        @pl.loop(0, tiles // 2)
        def _(double):
            number = double * 2
            add(pair, number, high_a, low_a)
            rotate(number + 1, high_b, low_b)
            add(pair, number + 1, high_b, low_b)
            rotate((number + 2) % tiles, high_a, low_a)

        @pl.when(first < wide_count - PAIR)
        def _():
            ready(first + 3)

    out = pltpu.make_async_copy(total, stacks_ref, out_sem.at[0])
    out.start()
    for slot in range(slots - PAIR, slots):
        wait_slot(slot)
        wait_source(slot)
    last = [
        pltpu.make_async_copy(spectra.at[pl.ds((slots - PAIR) * length, PAIR * length)], last_receiver_ref, out_sem.at[1]),
        pltpu.make_async_copy(sources.at[pl.ds(slots - PAIR, PAIR)], last_source_ref, out_sem.at[2]),
    ]
    for copy in last:
        copy.start()

    @pl.loop(0, forwarded)
    def _(slot):
        onward(slot).wait_send()

    @pl.loop(1, wide_count)
    def _(step):
        exchange(step).wait_send()

    for step in range(rep_count):
        if step < rep_count - 1:
            source_onward(step).wait_send()

        @pl.loop(1, wide_count)
        def _(number):
            source_share(step, number).wait_send()

    for copy in last:
        copy.wait()
    out.wait()


def gather_stacks(record, valid, picked, picked_valid, wide_count, rep_count):
    length, channels = record.shape
    bins = length // 2
    shard = channels // wide_count
    slots = wide_count * rep_count
    rows = picked.shape[1]
    lags = LAGS // rep_count
    band, inverse_count = band_matrix(bins)
    rotation = rotation_tables(length, bins)
    in_vmem = pl.BlockSpec(memory_space=pltpu.VMEM)
    anywhere = pl.BlockSpec(memory_space=pl.ANY)
    flops = 4 * lags * rows * slots * length * shard
    half = [pltpu.VMEM((TILE_LAGS * rows, PAIR * length), jnp.bfloat16), pltpu.VMEM((TILE_LAGS * rows, PAIR * length), jnp.float8_e5m2)]
    return pl.pallas_call(
        functools.partial(gather_kernel, wide_count, rep_count),
        in_specs=[anywhere] + [in_vmem] * 8,
        out_specs=[anywhere] * 3,
        out_shape=[
            jax.ShapeDtypeStruct((lags * rows, shard), jnp.float32),
            jax.ShapeDtypeStruct((PAIR * length, shard), jnp.bfloat16),
            jax.ShapeDtypeStruct((PAIR, rows, length), jnp.bfloat16),
        ],
        scratch_shapes=[
            pltpu.VMEM(((slots + wide_count - 1) * length, shard), jnp.bfloat16),
            pltpu.VMEM((slots, rows, length), jnp.bfloat16),
            pltpu.VMEM((lags * rows, shard), jnp.float32),
            pltpu.VMEM((PAIR * length, shard), jnp.float8_e5m2),
            *half,
            *half,
            pltpu.SemaphoreType.DMA((wide_count,)),
            pltpu.SemaphoreType.DMA((3,)),
            pltpu.SemaphoreType.DMA((slots,)),
            pltpu.SemaphoreType.DMA((slots,)),
            pltpu.SemaphoreType.DMA((rep_count,)),
            pltpu.SemaphoreType.DMA((slots,)),
            pltpu.SemaphoreType.DMA((slots,)),
        ],
        compiler_params=pltpu.CompilerParams(collective_id=0, has_side_effects=True, vmem_limit_bytes=VMEM_LIMIT),
        cost_estimate=pl.CostEstimate(flops=flops, bytes_accessed=lags * rows * shard * 4, transcendentals=0),
        name="gather_stacks",
    )(record, valid, picked, picked_valid, forward_table(length, bins), hann_window(length), band, inverse_count, rotation)


def last_kernel(scale, source_ref, rotation_ref, receiver_ref, before_ref, out_ref, high_ref, low_ref, coarse_ref):
    lags, rows, channels = out_ref.shape
    first_lag = (lax.axis_index("rep") * pl.num_programs(0) + pl.program_id(0)) * lags

    @pl.when(pl.program_id(0) == 0)
    def _():
        coarse_ref[...] = receiver_ref[...].astype(coarse_ref.dtype)

    rotate_split([source_ref[window] for window in range(source_ref.shape[0])], rotation_ref, first_lag, lags, high_ref, low_ref)
    tile = min(256, channels)
    for first in range(0, channels, tile):
        columns = slice(first, first + tile)
        value = jnp.dot(high_ref[...], receiver_ref[:, columns], preferred_element_type=jnp.float32)
        value = value + jnp.dot(low_ref[...], coarse_ref[:, columns], preferred_element_type=jnp.float32)
        value = (value + before_ref[:, columns]) * scale
        out_ref[:, :, columns] = value.reshape(lags, rows, tile)


def last_stacks(source, receiver, before, scale, rep_count):
    windows, rows, depth = source.shape
    channels = receiver.shape[1]
    lags = LAGS // rep_count
    rotation = rotation_tables(depth, depth // 2)
    return pl.pallas_call(
        functools.partial(last_kernel, scale),
        grid=(lags // LAST_TILE_LAGS,),
        in_specs=[
            pl.BlockSpec((windows, rows, depth), lambda i: (0, 0, 0)),
            pl.BlockSpec(rotation.shape, lambda i: (0, 0, 0)),
            pl.BlockSpec((windows * depth, channels), lambda i: (0, 0)),
            pl.BlockSpec((LAST_TILE_LAGS * rows, channels), lambda i: (i, 0)),
        ],
        out_specs=pl.BlockSpec((LAST_TILE_LAGS, rows, channels), lambda i: (i, 0, 0)),
        out_shape=jax.ShapeDtypeStruct((lags, rows, channels), jnp.float32),
        scratch_shapes=[
            pltpu.VMEM((LAST_TILE_LAGS * rows, windows * depth), jnp.bfloat16),
            pltpu.VMEM((LAST_TILE_LAGS * rows, windows * depth), jnp.float8_e5m2),
            pltpu.VMEM((windows * depth, channels), jnp.float8_e5m2),
        ],
        compiler_params=pltpu.CompilerParams(vmem_limit_bytes=VMEM_LIMIT),
        name="last_stacks",
    )(source, rotation, receiver, before)


def on_device(record, valid, sources):
    wide_count = lax.axis_size("wide")
    rep_count = lax.axis_size("rep")
    length = record.shape[1]
    starts = [sources[number] * SRC for number in range(sources.shape[0])]
    picked = jnp.concatenate([lax.dynamic_slice_in_dim(record[0], start, SRC, 1) for start in starts], axis=1)
    picked_valid = jnp.concatenate([lax.dynamic_slice_in_dim(valid, start, SRC, 1) for start in starts], axis=1)
    before, receiver, source = gather_stacks(record[0], valid, picked, picked_valid, wide_count, rep_count)
    scale = 1.0 / math.sqrt(wide_count * rep_count * (length // 2)) / RAISE
    return last_stacks(source, receiver, before, scale, rep_count)


def solution(mesh):
    return jax.shard_map(
        on_device,
        mesh=mesh,
        in_specs=(P(("wide", "rep"), None, None), P(("wide", "rep"), None), P()),
        out_specs=P("rep", None, "wide"),
        check_vma=False,
    )
```

```python
import functools
import math

import jax
import jax.numpy as jnp
import numpy as np
from jax import lax
from jax.experimental import pallas as pl
from jax.experimental.pallas import tpu as pltpu
from jax.sharding import PartitionSpec as P

SRC = 64
LAGS = 128
HALF_SMOOTH = 5
EPSILON = 1e-05
LEVEL_SHARE = 0.2

VMEM_LIMIT = 56 * 1024 * 1024
TILE_LAGS = 4
PAIR = 2
RAISE = 2.0**16
MESH = pl.DeviceIdType.MESH


def forward_table(length, bins):
    phase = 2.0 * math.pi / length * np.mod(np.outer(np.arange(1, bins + 1), np.arange(length)), length)
    return jnp.asarray(np.concatenate([np.cos(phase), -np.sin(phase)], axis=0), jnp.bfloat16)


def hann_window(length):
    return jnp.asarray(0.5 - 0.5 * np.cos(2.0 * math.pi / length * np.arange(length)), jnp.float32)[:, None]


def band_matrix(bins):
    rows = np.arange(bins)
    near = (np.abs(rows[:, None] - rows[None, :]) <= HALF_SMOOTH).astype(np.float32)
    return jnp.asarray(near, jnp.bfloat16), jnp.asarray(1.0 / near.sum(axis=1, keepdims=True), jnp.float32)


def rotation_tables(length, bins):
    shifts = np.arange(LAGS) - LAGS // 2
    phase = 2.0 * math.pi / length * np.mod(np.outer(shifts, np.arange(1, bins + 1)), length)
    return jnp.asarray(np.stack([np.cos(phase), np.sin(phase)], 1) * RAISE, jnp.float32)


def whiten_tile(samples, flags, table, taper, band, inverse_count):
    bins = band.shape[0]
    samples = samples.astype(jnp.float32)
    centered = samples - jnp.mean(samples, axis=0, keepdims=True)
    tapered = (centered * taper).astype(jnp.bfloat16)
    spectrum = jnp.dot(table, tapered, preferred_element_type=jnp.float32)
    real, imag = spectrum[:bins], spectrum[bins:]
    magnitude = jnp.sqrt(real * real + imag * imag)
    smooth = jnp.zeros_like(magnitude)
    rest = magnitude
    for _ in range(3):
        piece = rest.astype(jnp.bfloat16)
        rest = rest - piece.astype(jnp.float32)
        smooth = smooth + jnp.dot(band, piece, preferred_element_type=jnp.float32)
    smooth = smooth * inverse_count
    level = jnp.mean(magnitude, axis=0, keepdims=True)
    gain = flags.astype(jnp.float32) / (smooth + (LEVEL_SHARE * level + EPSILON))
    return real * gain, imag * gain


def rotate_split(source, rotation_ref, first_lag, lags, high_ref, low_ref):
    for window in range(len(source)):
        spectrum = source[window].astype(jnp.float32)
        rows, depth = spectrum.shape
        half = depth // 2
        real, imag = spectrum[:, :half], spectrum[:, half:]
        for lag in range(lags):
            cos, sin = rotation_ref[first_lag + lag, 0:1], rotation_ref[first_lag + lag, 1:2]
            for part, value in enumerate((real * cos + imag * sin, imag * cos - real * sin)):
                high = value.astype(jnp.bfloat16)
                column = window * depth + part * half
                at = (slice(lag * rows, (lag + 1) * rows), slice(column, column + half))
                high_ref[at] = high
                low_ref[at] = (value - high.astype(jnp.float32)).astype(low_ref.dtype)


def pick_kernel(blocks_ref, *refs):
    count = blocks_ref.shape[0]
    table_ref, taper_ref, band_ref, inverse_count_ref, out_ref = refs[2 * count :]
    real, imag = whiten_tile(
        jnp.concatenate([ref[...].astype(jnp.float32) for ref in refs[:count]], axis=1),
        jnp.concatenate([ref[...].astype(jnp.float32) for ref in refs[count : 2 * count]], axis=1),
        table_ref[...],
        taper_ref[...],
        band_ref[...],
        inverse_count_ref[...],
    )
    turned = jnp.concatenate([real, imag], axis=0).T
    for number in range(count):
        both = turned[number * 2 * SRC : (number + 1) * 2 * SRC]
        chosen = jnp.where(blocks_ref[number] % 2 == 1, both[SRC:], both[:SRC])
        out_ref[number * SRC : (number + 1) * SRC] = chosen.astype(jnp.bfloat16)


def pick_sources(record, valid, blocks):
    length = record.shape[0]
    bins = length // 2
    count = blocks.shape[0]
    band, inverse_count = band_matrix(bins)

    def block_specs(rows):
        return [pl.BlockSpec((rows, 2 * SRC), lambda i, at, number=number: (0, at[number] // 2)) for number in range(count)]

    in_vmem = pl.BlockSpec(memory_space=pltpu.VMEM)
    return pl.pallas_call(
        pick_kernel,
        grid_spec=pltpu.PrefetchScalarGridSpec(
            num_scalar_prefetch=1,
            grid=(1,),
            in_specs=block_specs(length) + block_specs(1) + [in_vmem] * 4,
            out_specs=pl.BlockSpec((count * SRC, length), lambda i, at: (0, 0)),
        ),
        out_shape=jax.ShapeDtypeStruct((count * SRC, length), jnp.bfloat16),
        name="pick_sources",
    )(blocks, *[record] * count, *[valid] * count, forward_table(length, bins), hann_window(length), band, inverse_count)


def gather_kernel(
    wide_count,
    rep_count,
    record_ref,
    valid_ref,
    picked_ref,
    table_ref,
    taper_ref,
    band_ref,
    inverse_count_ref,
    rotation_ref,
    total,
    last_receiver_ref,
    last_source_ref,
    raw,
    spectra,
    sources,
    coarse,
    high_a,
    low_a,
    high_b,
    low_b,
    raw_sem,
    send_sem,
    recv_sem,
    source_send_sem,
    source_recv_sem,
    share_sem,
):
    wide, rep = lax.axis_index("wide"), lax.axis_index("rep")
    slots = wide_count * rep_count
    forwarded = slots - wide_count
    length, shard = table_ref.shape[1], total.shape[1]
    rows = sources.shape[1]
    bits = wide_count.bit_length() - 1
    following = (wide, lax.rem(rep + 1, rep_count))
    preceding = (wide, lax.rem(rep + rep_count - 1, rep_count))

    def peer(step):
        index = 0
        for bit in range(bits):
            index = index + ((wide // 2**bit + step // 2**bit) % 2) * 2**bit
        return index

    def slot_rows(slot):
        return pl.ds(pl.multiple_of(slot * length, length), length)

    def shard_columns(step):
        return pl.ds(pl.multiple_of(peer(step) * shard, shard), shard)

    def spectra_copy(source, target, device, sem):
        return pltpu.make_async_remote_copy(
            src_ref=spectra.at[slot_rows(source)],
            dst_ref=spectra.at[slot_rows(target)],
            send_sem=send_sem.at[sem],
            recv_sem=recv_sem.at[target],
            device_id=device,
            device_id_type=MESH,
        )

    def onward(slot):
        return spectra_copy(slot, slot + wide_count, following, slot)

    def exchange(step):
        return pltpu.make_async_remote_copy(
            src_ref=raw.at[:, shard_columns(step)],
            dst_ref=spectra.at[slot_rows(step)],
            send_sem=send_sem.at[forwarded + step],
            recv_sem=recv_sem.at[step],
            device_id=(peer(step), rep),
            device_id_type=MESH,
        )

    def source_copy(source, target, device, sem):
        return pltpu.make_async_remote_copy(
            src_ref=sources.at[source],
            dst_ref=sources.at[target],
            send_sem=sem,
            recv_sem=source_recv_sem.at[target],
            device_id=device,
            device_id_type=MESH,
        )

    def source_onward(step):
        return source_copy(step * wide_count, (step + 1) * wide_count, following, source_send_sem.at[step])

    def source_share(step, number):
        slot = step * wide_count
        return source_copy(slot, slot + number, (peer(number), rep), share_sem.at[slot + number])

    def wait_slot(slot):
        spectra_copy(slot, slot, following, slot).wait_recv()

    def wait_source(slot):
        source_copy(slot, slot, following, share_sem.at[slot]).wait_recv()

    def ready(slot):
        wait_slot(slot)

        @pl.when(slot < forwarded)
        def _():
            onward(slot).start()

    def share_sources(step):
        if step:
            wait_source(step * wide_count)
        if step < rep_count - 1:
            source_onward(step).start()

        @pl.loop(1, wide_count)
        def _(number):
            source_share(step, number).start()

    def whiten(step, out_ref, out_column):
        tile = min(512, shard)
        bins = length // 2

        @pl.loop(0, shard // tile)
        def _(number):
            start = pl.multiple_of(peer(step) * shard + number * tile, tile)
            real, imag = whiten_tile(
                raw[:, pl.ds(start, tile)],
                valid_ref[:, pl.ds(start, tile)],
                table_ref[...],
                taper_ref[...],
                band_ref[...],
                inverse_count_ref[...],
            )
            columns = pl.ds(pl.multiple_of(out_column + number * tile, tile), tile)
            out_ref[:bins, columns] = real.astype(jnp.bfloat16)
            out_ref[bins : 2 * bins, columns] = imag.astype(jnp.bfloat16)

    record = pltpu.make_async_copy(record_ref, raw, raw_sem)
    record.start()
    barrier = pltpu.get_barrier_semaphore()
    pl.semaphore_signal(barrier, inc=1, device_id=preceding, device_id_type=MESH)

    @pl.loop(1, wide_count)
    def _(step):
        pl.semaphore_signal(barrier, inc=1, device_id=(peer(step), rep), device_id_type=MESH)

    sources[0] = picked_ref[...]
    pl.semaphore_wait(barrier, wide_count)
    share_sources(0)
    record.wait()
    whiten(0, spectra, 0)
    onward(0).start()

    @pl.loop(1, wide_count)
    def _(step):
        whiten(step, raw, peer(step) * shard)
        exchange(step).start()

        @pl.when(step == 3)
        def _():
            ready(1)
            share_sources(1)

    total[...] = jnp.zeros_like(total)

    lags = LAGS // rep_count
    tiles = lags // TILE_LAGS
    tile_rows = TILE_LAGS * rows
    tile = min(256, shard)

    def add(first, count, number, high_ref, low_ref):
        at = pl.ds(pl.multiple_of(number * tile_rows, tile_rows), tile_rows)
        depth = pl.ds(pl.multiple_of(first * length, length), count * length)
        for start in range(0, shard, tile):
            columns = slice(start, start + tile)
            value = jnp.dot(high_ref[:, : count * length], spectra[depth, columns], preferred_element_type=jnp.float32)
            low = low_ref[:, : count * length]
            value = value + jnp.dot(low, coarse[: count * length, columns], preferred_element_type=jnp.float32)
            total[at, columns] += value

    def add_windows(first, count):
        depth = pl.ds(pl.multiple_of(first * length, length), count * length)
        coarse[: count * length] = spectra[depth, :].astype(coarse.dtype)
        source = [sources.at[first + number] for number in range(count)]

        def rotate(number, high_ref, low_ref):
            rotate_split([ref[...] for ref in source], rotation_ref, rep * lags + number * TILE_LAGS, TILE_LAGS, high_ref, low_ref)

        rotate(0, high_a, low_a)

        @pl.loop(0, tiles // 2)
        def _(double):
            number = double * 2
            add(first, count, number, high_a, low_a)
            rotate(number + 1, high_b, low_b)
            add(first, count, number + 1, high_b, low_b)
            rotate((number + 2) % tiles, high_a, low_a)

    @pl.loop(0, slots // PAIR - 1)
    def _(pair):
        first = pair * PAIR

        @pl.when(first < wide_count - PAIR)
        def _():
            ready(first + 2)

        @pl.when(first >= wide_count)
        def _():
            ready(first)
            ready(first + 1)

        @pl.when(first % wide_count != 0)
        def _():
            wait_source(first)

        wait_source(first + 1)
        for step in range(2, rep_count):

            @pl.when(pair == step - 2)
            def _():
                share_sources(step)

        add_windows(first, PAIR)

        @pl.when(first < wide_count - PAIR)
        def _():
            ready(first + 3)

    wait_slot(slots - 2)
    wait_source(slots - 2)
    add_windows(slots - 2, 1)
    wait_slot(slots - 1)
    wait_source(slots - 1)
    last_receiver_ref[...] = spectra[(slots - 1) * length :]
    last_source_ref[...] = sources[slots - 1]

    @pl.loop(0, forwarded)
    def _(slot):
        onward(slot).wait_send()

    @pl.loop(1, wide_count)
    def _(step):
        exchange(step).wait_send()

    for step in range(rep_count):
        if step < rep_count - 1:
            source_onward(step).wait_send()

        @pl.loop(1, wide_count)
        def _(number):
            source_share(step, number).wait_send()


def gather_stacks(record, valid, picked, wide_count, rep_count):
    length, channels = record.shape
    bins = length // 2
    shard = channels // wide_count
    slots = wide_count * rep_count
    rows = picked.shape[0]
    lags = LAGS // rep_count
    band, inverse_count = band_matrix(bins)
    rotation = rotation_tables(length, bins)
    in_vmem = pl.BlockSpec(memory_space=pltpu.VMEM)
    flops = 4 * lags * rows * slots * length * shard
    half = [pltpu.VMEM((TILE_LAGS * rows, PAIR * length), jnp.bfloat16), pltpu.VMEM((TILE_LAGS * rows, PAIR * length), jnp.float8_e5m2)]
    return pl.pallas_call(
        functools.partial(gather_kernel, wide_count, rep_count),
        in_specs=[pl.BlockSpec(memory_space=pl.ANY)] + [in_vmem] * 7,
        out_specs=[in_vmem] * 3,
        out_shape=[
            pltpu.VMEM((lags * rows, shard), jnp.float32),
            jax.ShapeDtypeStruct((length, shard), jnp.bfloat16),
            jax.ShapeDtypeStruct((rows, length), jnp.bfloat16),
        ],
        scratch_shapes=[
            pltpu.VMEM((length, channels), jnp.bfloat16),
            pltpu.VMEM((slots * length, shard), jnp.bfloat16),
            pltpu.VMEM((slots, rows, length), jnp.bfloat16),
            pltpu.VMEM((PAIR * length, shard), jnp.float8_e5m2),
            *half,
            *half,
            pltpu.SemaphoreType.DMA,
            pltpu.SemaphoreType.DMA((slots,)),
            pltpu.SemaphoreType.DMA((slots,)),
            pltpu.SemaphoreType.DMA((rep_count,)),
            pltpu.SemaphoreType.DMA((slots,)),
            pltpu.SemaphoreType.DMA((slots,)),
        ],
        compiler_params=pltpu.CompilerParams(collective_id=0, has_side_effects=True, vmem_limit_bytes=VMEM_LIMIT - 4 * lags * rows * shard),
        cost_estimate=pl.CostEstimate(flops=flops, bytes_accessed=lags * rows * shard * 4, transcendentals=0),
        name="gather_stacks",
    )(record, valid, picked, forward_table(length, bins), hann_window(length), band, inverse_count, rotation)


def last_kernel(scale, source_ref, rotation_ref, receiver_ref, before_ref, out_ref, high_a, low_a, high_b, low_b, coarse, stage_a, stage_b, sem):
    lags, rows, channels = stage_a.shape
    tiles = out_ref.shape[0] // lags
    first_lag = lax.axis_index("rep") * out_ref.shape[0]
    tile = min(256, channels)
    coarse[...] = receiver_ref[...].astype(coarse.dtype)

    def rotate(number, high_ref, low_ref):
        rotate_split([source_ref[...]], rotation_ref, first_lag + number * lags, lags, high_ref, low_ref)

    def write(number, stage, at):
        return pltpu.make_async_copy(stage, out_ref.at[pl.ds(number * lags, lags)], sem.at[at])

    def finish(number, high_ref, low_ref, stage):
        at = pl.ds(pl.multiple_of(number * lags * rows, lags * rows), lags * rows)
        for start in range(0, channels, tile):
            columns = slice(start, start + tile)
            value = jnp.dot(high_ref[...], receiver_ref[:, columns], preferred_element_type=jnp.float32)
            value = value + jnp.dot(low_ref[...], coarse[:, columns], preferred_element_type=jnp.float32)
            value = (value + before_ref[at, columns]) * scale
            stage[:, :, columns] = value.reshape(lags, rows, tile)

    rotate(0, high_a, low_a)

    @pl.loop(0, tiles // 2)
    def _(double):
        number = double * 2

        @pl.when(double > 0)
        def _():
            write(number - 2, stage_a, 0).wait()

        finish(number, high_a, low_a, stage_a)
        write(number, stage_a, 0).start()
        rotate(number + 1, high_b, low_b)

        @pl.when(double > 0)
        def _():
            write(number - 1, stage_b, 1).wait()

        finish(number + 1, high_b, low_b, stage_b)
        write(number + 1, stage_b, 1).start()
        rotate((number + 2) % tiles, high_a, low_a)

    write(tiles - 2, stage_a, 0).wait()
    write(tiles - 1, stage_b, 1).wait()


def last_stacks(source, receiver, before, scale, rep_count):
    rows, length = source.shape
    channels = receiver.shape[1]
    in_vmem = pl.BlockSpec(memory_space=pltpu.VMEM)
    half = [pltpu.VMEM((TILE_LAGS * rows, length), jnp.bfloat16), pltpu.VMEM((TILE_LAGS * rows, length), jnp.float8_e5m2)]
    return pl.pallas_call(
        functools.partial(last_kernel, scale),
        in_specs=[in_vmem] * 4,
        out_specs=pl.BlockSpec(memory_space=pl.ANY),
        out_shape=jax.ShapeDtypeStruct((LAGS // rep_count, rows, channels), jnp.float32),
        scratch_shapes=[
            *half,
            *half,
            pltpu.VMEM((length, channels), jnp.float8_e5m2),
            pltpu.VMEM((TILE_LAGS, rows, channels), jnp.float32),
            pltpu.VMEM((TILE_LAGS, rows, channels), jnp.float32),
            pltpu.SemaphoreType.DMA((2,)),
        ],
        compiler_params=pltpu.CompilerParams(vmem_limit_bytes=VMEM_LIMIT - 4 * before.size),
        name="last_stacks",
    )(source, rotation_tables(length, length // 2), receiver, before)


def on_device(record, valid, sources):
    wide_count = lax.axis_size("wide")
    rep_count = lax.axis_size("rep")
    length = record.shape[1]
    picked = pick_sources(record[0], valid, sources)
    before, receiver, source = gather_stacks(record[0], valid, picked, wide_count, rep_count)
    scale = 1.0 / math.sqrt(wide_count * rep_count * (length // 2)) / RAISE
    before = pltpu.with_memory_space_constraint(before, pltpu.VMEM)
    return last_stacks(source, receiver, before, scale, rep_count)


def solution(mesh):
    return jax.shard_map(
        on_device,
        mesh=mesh,
        in_specs=(P(("wide", "rep"), None, None), P(("wide", "rep"), None), P()),
        out_specs=P("rep", None, "wide"),
        check_vma=False,
    )
```

```python
import functools
import math

import jax
import jax.numpy as jnp
import numpy as np
from jax import lax
from jax.experimental import pallas as pl
from jax.experimental.pallas import tpu as pltpu
from jax.sharding import PartitionSpec as P

SRC = 64
LAGS = 128
HALF_SMOOTH = 5
EPSILON = 1e-05
LEVEL_SHARE = 0.2

VMEM_LIMIT = 56 * 1024 * 1024
TILE_LAGS = 4
PAIR = 2
RAISE = 2.0**16
MESH = pl.DeviceIdType.MESH


def forward_table(length, bins):
    phase = 2.0 * math.pi / length * np.mod(np.outer(np.arange(1, bins + 1), np.arange(length)), length)
    return jnp.asarray(np.concatenate([np.cos(phase), -np.sin(phase)], axis=0), jnp.bfloat16)


def hann_window(length):
    return jnp.asarray(0.5 - 0.5 * np.cos(2.0 * math.pi / length * np.arange(length)), jnp.float32)[:, None]


def band_matrix(bins):
    rows = np.arange(bins)
    near = (np.abs(rows[:, None] - rows[None, :]) <= HALF_SMOOTH).astype(np.float32)
    return jnp.asarray(near, jnp.bfloat16), jnp.asarray(1.0 / near.sum(axis=1, keepdims=True), jnp.float32)


def rotation_tables(length, bins):
    shifts = np.arange(LAGS) - LAGS // 2
    phase = 2.0 * math.pi / length * np.mod(np.outer(shifts, np.arange(1, bins + 1)), length)
    return jnp.asarray(np.stack([np.cos(phase), np.sin(phase)], 1) * RAISE, jnp.float32)


def whiten_tile(samples, flags, table, taper, band, inverse_count):
    bins = band.shape[0]
    samples = samples.astype(jnp.float32)
    centered = samples - jnp.mean(samples, axis=0, keepdims=True)
    tapered = (centered * taper).astype(jnp.bfloat16)
    spectrum = jnp.dot(table, tapered, preferred_element_type=jnp.float32)
    real, imag = spectrum[:bins], spectrum[bins:]
    magnitude = jnp.sqrt(real * real + imag * imag)
    smooth = jnp.zeros_like(magnitude)
    rest = magnitude
    for _ in range(3):
        piece = rest.astype(jnp.bfloat16)
        rest = rest - piece.astype(jnp.float32)
        smooth = smooth + jnp.dot(band, piece, preferred_element_type=jnp.float32)
    smooth = smooth * inverse_count
    level = jnp.mean(magnitude, axis=0, keepdims=True)
    gain = flags.astype(jnp.float32) / (smooth + (LEVEL_SHARE * level + EPSILON))
    return real * gain, imag * gain


def rotate_split(source, rotation_ref, first_lag, lags, high_ref, low_ref):
    for window in range(len(source)):
        spectrum = source[window].astype(jnp.float32)
        rows, depth = spectrum.shape
        half = depth // 2
        real, imag = spectrum[:, :half], spectrum[:, half:]
        for lag in range(lags):
            cos, sin = rotation_ref[first_lag + lag, 0:1], rotation_ref[first_lag + lag, 1:2]
            for part, value in enumerate((real * cos + imag * sin, imag * cos - real * sin)):
                high = value.astype(jnp.bfloat16)
                column = window * depth + part * half
                at = (slice(lag * rows, (lag + 1) * rows), slice(column, column + half))
                high_ref[at] = high
                low_ref[at] = (value - high.astype(jnp.float32)).astype(low_ref.dtype)


def pick_kernel(blocks_ref, *refs):
    count = blocks_ref.shape[0]
    table_ref, taper_ref, band_ref, inverse_count_ref, out_ref = refs[2 * count :]
    real, imag = whiten_tile(
        jnp.concatenate([ref[...].astype(jnp.float32) for ref in refs[:count]], axis=1),
        jnp.concatenate([ref[...].astype(jnp.float32) for ref in refs[count : 2 * count]], axis=1),
        table_ref[...],
        taper_ref[...],
        band_ref[...],
        inverse_count_ref[...],
    )
    turned = jnp.concatenate([real, imag], axis=0).T
    for number in range(count):
        both = turned[number * 2 * SRC : (number + 1) * 2 * SRC]
        chosen = jnp.where(blocks_ref[number] % 2 == 1, both[SRC:], both[:SRC])
        out_ref[number * SRC : (number + 1) * SRC] = chosen.astype(jnp.bfloat16)


def pick_sources(record, valid, blocks):
    length = record.shape[0]
    bins = length // 2
    count = blocks.shape[0]
    band, inverse_count = band_matrix(bins)

    def block_specs(rows):
        return [pl.BlockSpec((rows, 2 * SRC), lambda i, at, number=number: (0, at[number] // 2)) for number in range(count)]

    in_vmem = pl.BlockSpec(memory_space=pltpu.VMEM)
    return pl.pallas_call(
        pick_kernel,
        grid_spec=pltpu.PrefetchScalarGridSpec(
            num_scalar_prefetch=1,
            grid=(1,),
            in_specs=block_specs(length) + block_specs(1) + [in_vmem] * 4,
            out_specs=pl.BlockSpec((count * SRC, length), lambda i, at: (0, 0)),
        ),
        out_shape=jax.ShapeDtypeStruct((count * SRC, length), jnp.bfloat16),
        name="pick_sources",
    )(blocks, *[record] * count, *[valid] * count, forward_table(length, bins), hann_window(length), band, inverse_count)


def gather_kernel(
    wide_count,
    rep_count,
    record_ref,
    valid_ref,
    picked_ref,
    table_ref,
    taper_ref,
    band_ref,
    inverse_count_ref,
    rotation_ref,
    total,
    last_receiver_ref,
    last_source_ref,
    raw,
    spectra,
    sources,
    coarse,
    high_a,
    low_a,
    high_b,
    low_b,
    raw_sem,
    send_sem,
    recv_sem,
    source_send_sem,
    source_recv_sem,
    share_sem,
):
    wide, rep = lax.axis_index("wide"), lax.axis_index("rep")
    slots = wide_count * rep_count
    forwarded = slots - wide_count
    length, shard = table_ref.shape[1], total.shape[1]
    rows = sources.shape[1]
    bits = wide_count.bit_length() - 1
    following = (wide, lax.rem(rep + 1, rep_count))
    preceding = (wide, lax.rem(rep + rep_count - 1, rep_count))

    def peer(step):
        index = 0
        for bit in range(bits):
            index = index + ((wide // 2**bit + step // 2**bit) % 2) * 2**bit
        return index

    def slot_rows(slot):
        return pl.ds(pl.multiple_of(slot * length, length), length)

    def shard_columns(step):
        return pl.ds(pl.multiple_of(peer(step) * shard, shard), shard)

    def raw_copy(step):
        columns = shard_columns(step)
        return pltpu.make_async_copy(record_ref.at[:, columns], raw.at[:, columns], raw_sem.at[step])

    def spectra_copy(source, target, device, sem):
        return pltpu.make_async_remote_copy(
            src_ref=spectra.at[slot_rows(source)],
            dst_ref=spectra.at[slot_rows(target)],
            send_sem=send_sem.at[sem],
            recv_sem=recv_sem.at[target],
            device_id=device,
            device_id_type=MESH,
        )

    def onward(slot):
        return spectra_copy(slot, slot + wide_count, following, slot)

    def exchange(step):
        return pltpu.make_async_remote_copy(
            src_ref=raw.at[:, shard_columns(step)],
            dst_ref=spectra.at[slot_rows(step)],
            send_sem=send_sem.at[forwarded + step],
            recv_sem=recv_sem.at[step],
            device_id=(peer(step), rep),
            device_id_type=MESH,
        )

    def source_copy(source, target, device, sem):
        return pltpu.make_async_remote_copy(
            src_ref=sources.at[source],
            dst_ref=sources.at[target],
            send_sem=sem,
            recv_sem=source_recv_sem.at[target],
            device_id=device,
            device_id_type=MESH,
        )

    def source_onward(step):
        return source_copy(step * wide_count, (step + 1) * wide_count, following, source_send_sem.at[step])

    def source_share(step, number):
        slot = step * wide_count
        return source_copy(slot, slot + number, (peer(number), rep), share_sem.at[slot + number])

    def wait_slot(slot):
        spectra_copy(slot, slot, following, slot).wait_recv()

    def wait_source(slot):
        source_copy(slot, slot, following, share_sem.at[slot]).wait_recv()

    def ready(slot):
        wait_slot(slot)

        @pl.when(slot < forwarded)
        def _():
            onward(slot).start()

    def share_sources(step):
        if step:
            wait_source(step * wide_count)
        if step < rep_count - 1:
            source_onward(step).start()

        @pl.loop(1, wide_count)
        def _(number):
            source_share(step, number).start()

    def whiten(step, out_ref, out_column):
        tile = min(512, shard)
        bins = length // 2

        @pl.loop(0, shard // tile)
        def _(number):
            start = pl.multiple_of(peer(step) * shard + number * tile, tile)
            real, imag = whiten_tile(
                raw[:, pl.ds(start, tile)],
                valid_ref[:, pl.ds(start, tile)],
                table_ref[...],
                taper_ref[...],
                band_ref[...],
                inverse_count_ref[...],
            )
            columns = pl.ds(pl.multiple_of(out_column + number * tile, tile), tile)
            out_ref[:bins, columns] = real.astype(jnp.bfloat16)
            out_ref[bins : 2 * bins, columns] = imag.astype(jnp.bfloat16)

    @pl.loop(0, wide_count)
    def _(step):
        raw_copy(step).start()

    barrier = pltpu.get_barrier_semaphore()
    pl.semaphore_signal(barrier, inc=1, device_id=preceding, device_id_type=MESH)

    @pl.loop(1, wide_count)
    def _(step):
        pl.semaphore_signal(barrier, inc=1, device_id=(peer(step), rep), device_id_type=MESH)

    sources[0] = picked_ref[...]
    pl.semaphore_wait(barrier, wide_count)
    share_sources(0)
    raw_copy(0).wait()
    whiten(0, spectra, 0)
    onward(0).start()

    @pl.loop(1, wide_count)
    def _(step):
        raw_copy(step).wait()
        whiten(step, raw, peer(step) * shard)
        exchange(step).start()

        @pl.when(step == 3)
        def _():
            ready(1)
            share_sources(1)

    total[...] = jnp.zeros_like(total)

    lags = LAGS // rep_count
    tiles = lags // TILE_LAGS
    tile_rows = TILE_LAGS * rows
    tile = min(256, shard)

    def add(first, count, number, high_ref, low_ref):
        at = pl.ds(pl.multiple_of(number * tile_rows, tile_rows), tile_rows)
        depth = pl.ds(pl.multiple_of(first * length, length), count * length)
        for start in range(0, shard, tile):
            columns = slice(start, start + tile)
            value = jnp.dot(high_ref[:, : count * length], spectra[depth, columns], preferred_element_type=jnp.float32)
            low = low_ref[:, : count * length]
            value = value + jnp.dot(low, coarse[: count * length, columns], preferred_element_type=jnp.float32)
            total[at, columns] += value

    def add_windows(first, count):
        depth = pl.ds(pl.multiple_of(first * length, length), count * length)
        coarse[: count * length] = spectra[depth, :].astype(coarse.dtype)
        source = [sources.at[first + number] for number in range(count)]

        def rotate(number, high_ref, low_ref):
            rotate_split([ref[...] for ref in source], rotation_ref, rep * lags + number * TILE_LAGS, TILE_LAGS, high_ref, low_ref)

        rotate(0, high_a, low_a)

        @pl.loop(0, tiles // 2)
        def _(double):
            number = double * 2
            add(first, count, number, high_a, low_a)
            rotate(number + 1, high_b, low_b)
            add(first, count, number + 1, high_b, low_b)
            rotate((number + 2) % tiles, high_a, low_a)

    @pl.loop(0, slots // PAIR - 1)
    def _(pair):
        first = pair * PAIR

        @pl.when(first < wide_count - PAIR)
        def _():
            ready(first + 2)

        @pl.when(first >= wide_count)
        def _():
            ready(first)
            ready(first + 1)

        @pl.when(first % wide_count != 0)
        def _():
            wait_source(first)

        wait_source(first + 1)
        for step in range(2, rep_count):

            @pl.when(pair == step - 2)
            def _():
                share_sources(step)

        add_windows(first, PAIR)

        @pl.when(first < wide_count - PAIR)
        def _():
            ready(first + 3)

    @pl.loop(1, wide_count)
    def _(step):
        exchange(step).wait_send()

    for step in range(rep_count):
        if step < rep_count - 1:
            source_onward(step).wait_send()

        @pl.loop(1, wide_count)
        def _(number):
            source_share(step, number).wait_send()

    @pl.loop(0, forwarded - 4)
    def _(slot):
        onward(slot).wait_send()

    wait_slot(slots - 2)
    wait_source(slots - 2)
    add_windows(slots - 2, 1)
    wait_slot(slots - 1)
    wait_source(slots - 1)
    last_receiver_ref[...] = spectra[(slots - 1) * length :]
    last_source_ref[...] = sources[slots - 1]

    @pl.loop(forwarded - 4, forwarded)
    def _(slot):
        onward(slot).wait_send()


def gather_stacks(record, valid, picked, wide_count, rep_count):
    length, channels = record.shape
    bins = length // 2
    shard = channels // wide_count
    slots = wide_count * rep_count
    rows = picked.shape[0]
    lags = LAGS // rep_count
    band, inverse_count = band_matrix(bins)
    rotation = rotation_tables(length, bins)
    in_vmem = pl.BlockSpec(memory_space=pltpu.VMEM)
    flops = 4 * lags * rows * slots * length * shard
    half = [pltpu.VMEM((TILE_LAGS * rows, PAIR * length), jnp.bfloat16), pltpu.VMEM((TILE_LAGS * rows, PAIR * length), jnp.float8_e5m2)]
    return pl.pallas_call(
        functools.partial(gather_kernel, wide_count, rep_count),
        in_specs=[pl.BlockSpec(memory_space=pl.ANY)] + [in_vmem] * 7,
        out_specs=[in_vmem] * 3,
        out_shape=[
            pltpu.VMEM((lags * rows, shard), jnp.float32),
            pltpu.VMEM((length, shard), jnp.bfloat16),
            pltpu.VMEM((rows, length), jnp.bfloat16),
        ],
        scratch_shapes=[
            pltpu.VMEM((length, channels), jnp.bfloat16),
            pltpu.VMEM((slots * length, shard), jnp.bfloat16),
            pltpu.VMEM((slots, rows, length), jnp.bfloat16),
            pltpu.VMEM((PAIR * length, shard), jnp.float8_e5m2),
            *half,
            *half,
            pltpu.SemaphoreType.DMA((wide_count,)),
            pltpu.SemaphoreType.DMA((slots,)),
            pltpu.SemaphoreType.DMA((slots,)),
            pltpu.SemaphoreType.DMA((rep_count,)),
            pltpu.SemaphoreType.DMA((slots,)),
            pltpu.SemaphoreType.DMA((slots,)),
        ],
        compiler_params=pltpu.CompilerParams(collective_id=0, has_side_effects=True, vmem_limit_bytes=VMEM_LIMIT - 4 * lags * rows * shard),
        cost_estimate=pl.CostEstimate(flops=flops, bytes_accessed=lags * rows * shard * 4, transcendentals=0),
        name="gather_stacks",
    )(record, valid, picked, forward_table(length, bins), hann_window(length), band, inverse_count, rotation)


def last_kernel(scale, source_ref, rotation_ref, receiver_ref, before_ref, out_ref, high_a, low_a, high_b, low_b, coarse, stage_a, stage_b, sem):
    lags, rows, channels = stage_a.shape
    tiles = out_ref.shape[0] // lags
    first_lag = lax.axis_index("rep") * out_ref.shape[0]
    tile = min(256, channels)
    coarse[...] = receiver_ref[...].astype(coarse.dtype)

    def rotate(number, high_ref, low_ref):
        rotate_split([source_ref[...]], rotation_ref, first_lag + number * lags, lags, high_ref, low_ref)

    def write(number, stage, at, part):
        columns = pl.ds(part * tile, tile)
        return pltpu.make_async_copy(stage.at[:, :, columns], out_ref.at[pl.ds(number * lags, lags), :, columns], sem.at[at, part])

    def wait_write(number, stage, at):
        for part in range(channels // tile):
            write(number, stage, at, part).wait()

    def finish(number, high_ref, low_ref, stage, side):
        at = pl.ds(pl.multiple_of(number * lags * rows, lags * rows), lags * rows)
        for start in range(0, channels, tile):
            columns = slice(start, start + tile)
            value = jnp.dot(high_ref[...], receiver_ref[:, columns], preferred_element_type=jnp.float32)
            value = value + jnp.dot(low_ref[...], coarse[:, columns], preferred_element_type=jnp.float32)
            value = (value + before_ref[at, columns]) * scale
            stage[:, :, columns] = value.reshape(lags, rows, tile)
            write(number, stage, side, start // tile).start()

    rotate(0, high_a, low_a)

    @pl.loop(0, tiles // 2)
    def _(double):
        number = double * 2

        @pl.when(double > 0)
        def _():
            wait_write(number - 2, stage_a, 0)

        finish(number, high_a, low_a, stage_a, 0)
        rotate(number + 1, high_b, low_b)

        @pl.when(double > 0)
        def _():
            wait_write(number - 1, stage_b, 1)

        finish(number + 1, high_b, low_b, stage_b, 1)
        rotate((number + 2) % tiles, high_a, low_a)

    wait_write(tiles - 2, stage_a, 0)
    wait_write(tiles - 1, stage_b, 1)


def last_stacks(source, receiver, before, scale, rep_count):
    rows, length = source.shape
    channels = receiver.shape[1]
    in_vmem = pl.BlockSpec(memory_space=pltpu.VMEM)
    half = [pltpu.VMEM((TILE_LAGS * rows, length), jnp.bfloat16), pltpu.VMEM((TILE_LAGS * rows, length), jnp.float8_e5m2)]
    return pl.pallas_call(
        functools.partial(last_kernel, scale),
        in_specs=[in_vmem] * 4,
        out_specs=pl.BlockSpec(memory_space=pl.ANY),
        out_shape=jax.ShapeDtypeStruct((LAGS // rep_count, rows, channels), jnp.float32),
        scratch_shapes=[
            *half,
            *half,
            pltpu.VMEM((length, channels), jnp.float8_e5m2),
            pltpu.VMEM((TILE_LAGS, rows, channels), jnp.float32),
            pltpu.VMEM((TILE_LAGS, rows, channels), jnp.float32),
            pltpu.SemaphoreType.DMA((2, channels // min(256, channels))),
        ],
        compiler_params=pltpu.CompilerParams(vmem_limit_bytes=VMEM_LIMIT - 4 * before.size),
        name="last_stacks",
    )(source, rotation_tables(length, length // 2), receiver, before)


def on_device(record, valid, sources):
    wide_count = lax.axis_size("wide")
    rep_count = lax.axis_size("rep")
    length = record.shape[1]
    picked = pick_sources(record[0], valid, sources)
    before, receiver, source = gather_stacks(record[0], valid, picked, wide_count, rep_count)
    scale = 1.0 / math.sqrt(wide_count * rep_count * (length // 2)) / RAISE
    before, receiver, source = (pltpu.with_memory_space_constraint(kept, pltpu.VMEM) for kept in (before, receiver, source))
    return last_stacks(source, receiver, before, scale, rep_count)


def solution(mesh):
    return jax.shard_map(
        on_device,
        mesh=mesh,
        in_specs=(P(("wide", "rep"), None, None), P(("wide", "rep"), None), P()),
        out_specs=P("rep", None, "wide"),
        check_vma=False,
    )
```

```python
import functools
import math

import jax
import jax.numpy as jnp
import numpy as np
from jax import lax
from jax.experimental import pallas as pl
from jax.experimental.pallas import tpu as pltpu
from jax.sharding import PartitionSpec as P

SRC = 64
LAGS = 128
HALF_SMOOTH = 5
EPSILON = 1e-05
LEVEL_SHARE = 0.2

VMEM_LIMIT = 56 * 1024 * 1024
TILE_LAGS = 4
LAST_TILE_LAGS = 8
PAIR = 2
RAISE = 2.0**16
MESH = pl.DeviceIdType.MESH


def forward_table(length, bins):
    phase = 2.0 * math.pi / length * np.mod(np.outer(np.arange(1, bins + 1), np.arange(length)), length)
    return jnp.asarray(np.concatenate([np.cos(phase), -np.sin(phase)], axis=0), jnp.bfloat16)


def hann_window(length):
    return jnp.asarray(0.5 - 0.5 * np.cos(2.0 * math.pi / length * np.arange(length)), jnp.float32)[:, None]


def band_matrix(bins):
    rows = np.arange(bins)
    near = (np.abs(rows[:, None] - rows[None, :]) <= HALF_SMOOTH).astype(np.float32)
    return jnp.asarray(near, jnp.bfloat16), jnp.asarray(1.0 / near.sum(axis=1, keepdims=True), jnp.float32)


def rotation_tables(length, bins):
    shifts = np.arange(LAGS) - LAGS // 2
    phase = 2.0 * math.pi / length * np.mod(np.outer(shifts, np.arange(1, bins + 1)), length)
    return jnp.asarray(np.stack([np.cos(phase), np.sin(phase)], 1) * RAISE, jnp.float32)


def whiten_tile(samples, flags, table, taper, band, inverse_count):
    bins = band.shape[0]
    samples = samples.astype(jnp.float32)
    centered = samples - jnp.mean(samples, axis=0, keepdims=True)
    tapered = (centered * taper).astype(jnp.bfloat16)
    spectrum = jnp.dot(table, tapered, preferred_element_type=jnp.float32)
    real, imag = spectrum[:bins], spectrum[bins:]
    magnitude = jnp.sqrt(real * real + imag * imag)
    smooth = jnp.zeros_like(magnitude)
    rest = magnitude
    for _ in range(3):
        piece = rest.astype(jnp.bfloat16)
        rest = rest - piece.astype(jnp.float32)
        smooth = smooth + jnp.dot(band, piece, preferred_element_type=jnp.float32)
    smooth = smooth * inverse_count
    level = jnp.mean(magnitude, axis=0, keepdims=True)
    gain = flags.astype(jnp.float32) / (smooth + (LEVEL_SHARE * level + EPSILON))
    return real * gain, imag * gain


def rotate_split(source, rotation_ref, first_lag, lags, high_ref, low_ref):
    for window in range(len(source)):
        spectrum = source[window].astype(jnp.float32)
        rows, depth = spectrum.shape
        half = depth // 2
        real, imag = spectrum[:, :half], spectrum[:, half:]
        for lag in range(lags):
            cos, sin = rotation_ref[first_lag + lag, 0:1], rotation_ref[first_lag + lag, 1:2]
            for part, value in enumerate((real * cos + imag * sin, imag * cos - real * sin)):
                high = value.astype(jnp.bfloat16)
                column = window * depth + part * half
                at = (slice(lag * rows, (lag + 1) * rows), slice(column, column + half))
                high_ref[at] = high
                low_ref[at] = (value - high.astype(jnp.float32)).astype(low_ref.dtype)


def pick_kernel(blocks_ref, *refs):
    count = blocks_ref.shape[0]
    table_ref, taper_ref, band_ref, inverse_count_ref, out_ref = refs[2 * count :]
    real, imag = whiten_tile(
        jnp.concatenate([ref[...].astype(jnp.float32) for ref in refs[:count]], axis=1),
        jnp.concatenate([ref[...].astype(jnp.float32) for ref in refs[count : 2 * count]], axis=1),
        table_ref[...],
        taper_ref[...],
        band_ref[...],
        inverse_count_ref[...],
    )
    turned = jnp.concatenate([real, imag], axis=0).T
    for number in range(count):
        both = turned[number * 2 * SRC : (number + 1) * 2 * SRC]
        chosen = jnp.where(blocks_ref[number] % 2 == 1, both[SRC:], both[:SRC])
        out_ref[number * SRC : (number + 1) * SRC] = chosen.astype(jnp.bfloat16)


def pick_sources(record, valid, blocks):
    length = record.shape[0]
    bins = length // 2
    count = blocks.shape[0]
    band, inverse_count = band_matrix(bins)

    def block_specs(rows):
        return [pl.BlockSpec((rows, 2 * SRC), lambda i, at, number=number: (0, at[number] // 2)) for number in range(count)]

    in_vmem = pl.BlockSpec(memory_space=pltpu.VMEM)
    return pl.pallas_call(
        pick_kernel,
        grid_spec=pltpu.PrefetchScalarGridSpec(
            num_scalar_prefetch=1,
            grid=(1,),
            in_specs=block_specs(length) + block_specs(1) + [in_vmem] * 4,
            out_specs=pl.BlockSpec((count * SRC, length), lambda i, at: (0, 0)),
        ),
        out_shape=jax.ShapeDtypeStruct((count * SRC, length), jnp.bfloat16),
        name="pick_sources",
    )(blocks, *[record] * count, *[valid] * count, forward_table(length, bins), hann_window(length), band, inverse_count)


def gather_kernel(
    wide_count,
    rep_count,
    record_ref,
    valid_ref,
    picked_ref,
    table_ref,
    taper_ref,
    band_ref,
    inverse_count_ref,
    rotation_ref,
    total,
    last_receiver_ref,
    last_source_ref,
    raw,
    spectra,
    sources,
    coarse,
    high_a,
    low_a,
    high_b,
    low_b,
    raw_sem,
    send_sem,
    recv_sem,
    source_send_sem,
    source_recv_sem,
    share_sem,
):
    wide, rep = lax.axis_index("wide"), lax.axis_index("rep")
    slots = wide_count * rep_count
    forwarded = slots - wide_count
    length, shard = table_ref.shape[1], total.shape[1]
    rows = sources.shape[1]
    bits = wide_count.bit_length() - 1
    following = (wide, lax.rem(rep + 1, rep_count))
    preceding = (wide, lax.rem(rep + rep_count - 1, rep_count))

    def peer(step):
        index = 0
        for bit in range(bits):
            index = index + ((wide // 2**bit + step // 2**bit) % 2) * 2**bit
        return index

    def slot_rows(slot):
        return pl.ds(pl.multiple_of(slot * length, length), length)

    def shard_columns(step):
        return pl.ds(pl.multiple_of(peer(step) * shard, shard), shard)

    def raw_copy(step):
        columns = shard_columns(step)
        return pltpu.make_async_copy(record_ref.at[:, columns], raw.at[:, columns], raw_sem.at[step])

    def spectra_copy(source, target, device, sem):
        return pltpu.make_async_remote_copy(
            src_ref=spectra.at[slot_rows(source)],
            dst_ref=spectra.at[slot_rows(target)],
            send_sem=send_sem.at[sem],
            recv_sem=recv_sem.at[target],
            device_id=device,
            device_id_type=MESH,
        )

    def onward(slot):
        return spectra_copy(slot, slot + wide_count, following, slot)

    def exchange(step):
        return pltpu.make_async_remote_copy(
            src_ref=raw.at[:, shard_columns(step)],
            dst_ref=spectra.at[slot_rows(step)],
            send_sem=send_sem.at[forwarded + step],
            recv_sem=recv_sem.at[step],
            device_id=(peer(step), rep),
            device_id_type=MESH,
        )

    def source_copy(source, target, device, sem):
        return pltpu.make_async_remote_copy(
            src_ref=sources.at[source],
            dst_ref=sources.at[target],
            send_sem=sem,
            recv_sem=source_recv_sem.at[target],
            device_id=device,
            device_id_type=MESH,
        )

    def source_onward(step):
        return source_copy(step * wide_count, (step + 1) * wide_count, following, source_send_sem.at[step])

    def source_share(step, number):
        slot = step * wide_count
        return source_copy(slot, slot + number, (peer(number), rep), share_sem.at[slot + number])

    def wait_slot(slot):
        spectra_copy(slot, slot, following, slot).wait_recv()

    def wait_source(slot):
        source_copy(slot, slot, following, share_sem.at[slot]).wait_recv()

    def ready(slot):
        wait_slot(slot)

        @pl.when(slot < forwarded)
        def _():
            onward(slot).start()

    def share_sources(step):
        if step:
            wait_source(step * wide_count)
        if step < rep_count - 1:
            source_onward(step).start()

        @pl.loop(1, wide_count)
        def _(number):
            source_share(step, number).start()

    def whiten(step, out_ref, out_column):
        tile = min(512, shard)
        bins = length // 2

        @pl.loop(0, shard // tile)
        def _(number):
            start = pl.multiple_of(peer(step) * shard + number * tile, tile)
            real, imag = whiten_tile(
                raw[:, pl.ds(start, tile)],
                valid_ref[:, pl.ds(start, tile)],
                table_ref[...],
                taper_ref[...],
                band_ref[...],
                inverse_count_ref[...],
            )
            columns = pl.ds(pl.multiple_of(out_column + number * tile, tile), tile)
            out_ref[:bins, columns] = real.astype(jnp.bfloat16)
            out_ref[bins : 2 * bins, columns] = imag.astype(jnp.bfloat16)

    @pl.loop(0, wide_count)
    def _(step):
        raw_copy(step).start()

    barrier = pltpu.get_barrier_semaphore()
    pl.semaphore_signal(barrier, inc=1, device_id=preceding, device_id_type=MESH)

    @pl.loop(1, wide_count)
    def _(step):
        pl.semaphore_signal(barrier, inc=1, device_id=(peer(step), rep), device_id_type=MESH)

    sources[0] = picked_ref[...]
    pl.semaphore_wait(barrier, wide_count)
    share_sources(0)
    raw_copy(0).wait()
    whiten(0, spectra, 0)
    onward(0).start()

    @pl.loop(1, wide_count)
    def _(step):
        raw_copy(step).wait()
        whiten(step, raw, peer(step) * shard)
        exchange(step).start()

        @pl.when(step == 3)
        def _():
            ready(1)
            share_sources(1)

    total[...] = jnp.zeros_like(total)

    lags = LAGS // rep_count
    tiles = lags // TILE_LAGS
    tile_rows = TILE_LAGS * rows
    tile = min(256, shard)

    def add(first, count, number, high_ref, low_ref):
        at = pl.ds(pl.multiple_of(number * tile_rows, tile_rows), tile_rows)
        depth = pl.ds(pl.multiple_of(first * length, length), count * length)
        for start in range(0, shard, tile):
            columns = slice(start, start + tile)
            value = jnp.dot(high_ref[:, : count * length], spectra[depth, columns], preferred_element_type=jnp.float32)
            low = low_ref[:, : count * length]
            value = value + jnp.dot(low, coarse[: count * length, columns], preferred_element_type=jnp.float32)
            total[at, columns] += value

    def add_windows(first, count):
        depth = pl.ds(pl.multiple_of(first * length, length), count * length)
        coarse[: count * length] = spectra[depth, :].astype(coarse.dtype)
        source = [sources.at[first + number] for number in range(count)]

        def rotate(number, high_ref, low_ref):
            rotate_split([ref[...] for ref in source], rotation_ref, rep * lags + number * TILE_LAGS, TILE_LAGS, high_ref, low_ref)

        rotate(0, high_a, low_a)

        @pl.loop(0, tiles // 2)
        def _(double):
            number = double * 2
            add(first, count, number, high_a, low_a)
            rotate(number + 1, high_b, low_b)
            add(first, count, number + 1, high_b, low_b)
            rotate((number + 2) % tiles, high_a, low_a)

    @pl.loop(0, slots // PAIR - 1)
    def _(pair):
        first = pair * PAIR

        @pl.when(first < wide_count - PAIR)
        def _():
            ready(first + 2)

        @pl.when(first >= wide_count)
        def _():
            ready(first)
            ready(first + 1)

        @pl.when(first % wide_count != 0)
        def _():
            wait_source(first)

        wait_source(first + 1)
        for step in range(2, rep_count):

            @pl.when(pair == step - 2)
            def _():
                share_sources(step)

        add_windows(first, PAIR)

        @pl.when(first < wide_count - PAIR)
        def _():
            ready(first + 3)

    @pl.loop(1, wide_count)
    def _(step):
        exchange(step).wait_send()

    for step in range(rep_count):
        if step < rep_count - 1:
            source_onward(step).wait_send()

        @pl.loop(1, wide_count)
        def _(number):
            source_share(step, number).wait_send()

    @pl.loop(0, forwarded - 4)
    def _(slot):
        onward(slot).wait_send()

    wait_slot(slots - 2)
    wait_source(slots - 2)
    add_windows(slots - 2, 1)
    wait_slot(slots - 1)
    wait_source(slots - 1)
    last_receiver_ref[...] = spectra[(slots - 1) * length :]
    last_source_ref[...] = sources[slots - 1]

    @pl.loop(forwarded - 4, forwarded)
    def _(slot):
        onward(slot).wait_send()


def gather_stacks(record, valid, picked, wide_count, rep_count):
    length, channels = record.shape
    bins = length // 2
    shard = channels // wide_count
    slots = wide_count * rep_count
    rows = picked.shape[0]
    lags = LAGS // rep_count
    band, inverse_count = band_matrix(bins)
    rotation = rotation_tables(length, bins)
    in_vmem = pl.BlockSpec(memory_space=pltpu.VMEM)
    flops = 4 * lags * rows * slots * length * shard
    half = [pltpu.VMEM((TILE_LAGS * rows, PAIR * length), jnp.bfloat16), pltpu.VMEM((TILE_LAGS * rows, PAIR * length), jnp.float8_e5m2)]
    return pl.pallas_call(
        functools.partial(gather_kernel, wide_count, rep_count),
        in_specs=[pl.BlockSpec(memory_space=pl.ANY)] + [in_vmem] * 7,
        out_specs=[in_vmem] * 3,
        out_shape=[
            pltpu.VMEM((lags * rows, shard), jnp.float32),
            pltpu.VMEM((length, shard), jnp.bfloat16),
            pltpu.VMEM((rows, length), jnp.bfloat16),
        ],
        scratch_shapes=[
            pltpu.VMEM((length, channels), jnp.bfloat16),
            pltpu.VMEM((slots * length, shard), jnp.bfloat16),
            pltpu.VMEM((slots, rows, length), jnp.bfloat16),
            pltpu.VMEM((PAIR * length, shard), jnp.float8_e5m2),
            *half,
            *half,
            pltpu.SemaphoreType.DMA((wide_count,)),
            pltpu.SemaphoreType.DMA((slots,)),
            pltpu.SemaphoreType.DMA((slots,)),
            pltpu.SemaphoreType.DMA((rep_count,)),
            pltpu.SemaphoreType.DMA((slots,)),
            pltpu.SemaphoreType.DMA((slots,)),
        ],
        compiler_params=pltpu.CompilerParams(collective_id=0, has_side_effects=True, vmem_limit_bytes=VMEM_LIMIT - 4 * lags * rows * shard),
        cost_estimate=pl.CostEstimate(flops=flops, bytes_accessed=lags * rows * shard * 4, transcendentals=0),
        name="gather_stacks",
    )(record, valid, picked, forward_table(length, bins), hann_window(length), band, inverse_count, rotation)


def last_kernel(scale, source_ref, rotation_ref, receiver_ref, before_ref, out_ref, high_a, low_a, high_b, low_b, coarse, stage_a, stage_b, sem):
    lags, rows, channels = stage_a.shape
    tiles = out_ref.shape[0] // lags
    first_lag = lax.axis_index("rep") * out_ref.shape[0]
    tile = min(256, channels)
    coarse[...] = receiver_ref[...].astype(coarse.dtype)

    def rotate(number, high_ref, low_ref):
        rotate_split([source_ref[...]], rotation_ref, first_lag + number * lags, lags, high_ref, low_ref)

    def write(number, stage, at, part):
        columns = pl.ds(part * tile, tile)
        return pltpu.make_async_copy(stage.at[:, :, columns], out_ref.at[pl.ds(number * lags, lags), :, columns], sem.at[at, part])

    def wait_write(number, stage, at):
        for part in range(channels // tile):
            write(number, stage, at, part).wait()

    def finish(number, high_ref, low_ref, stage, side):
        at = pl.ds(pl.multiple_of(number * lags * rows, lags * rows), lags * rows)
        for start in range(0, channels, tile):
            columns = slice(start, start + tile)
            value = jnp.dot(high_ref[...], receiver_ref[:, columns], preferred_element_type=jnp.float32)
            value = value + jnp.dot(low_ref[...], coarse[:, columns], preferred_element_type=jnp.float32)
            value = (value + before_ref[at, columns]) * scale
            stage[:, :, columns] = value.reshape(lags, rows, tile)
            write(number, stage, side, start // tile).start()

    rotate(0, high_a, low_a)

    @pl.loop(0, tiles // 2)
    def _(double):
        number = double * 2

        @pl.when(double > 0)
        def _():
            wait_write(number - 2, stage_a, 0)

        finish(number, high_a, low_a, stage_a, 0)
        rotate(number + 1, high_b, low_b)

        @pl.when(double > 0)
        def _():
            wait_write(number - 1, stage_b, 1)

        finish(number + 1, high_b, low_b, stage_b, 1)
        rotate((number + 2) % tiles, high_a, low_a)

    wait_write(tiles - 2, stage_a, 0)
    wait_write(tiles - 1, stage_b, 1)


def last_stacks(source, receiver, before, scale, rep_count):
    rows, length = source.shape
    channels = receiver.shape[1]
    in_vmem = pl.BlockSpec(memory_space=pltpu.VMEM)
    half = [pltpu.VMEM((LAST_TILE_LAGS * rows, length), jnp.bfloat16), pltpu.VMEM((LAST_TILE_LAGS * rows, length), jnp.float8_e5m2)]
    return pl.pallas_call(
        functools.partial(last_kernel, scale),
        in_specs=[in_vmem] * 4,
        out_specs=pl.BlockSpec(memory_space=pl.ANY),
        out_shape=jax.ShapeDtypeStruct((LAGS // rep_count, rows, channels), jnp.float32),
        scratch_shapes=[
            *half,
            *half,
            pltpu.VMEM((length, channels), jnp.float8_e5m2),
            pltpu.VMEM((LAST_TILE_LAGS, rows, channels), jnp.float32),
            pltpu.VMEM((LAST_TILE_LAGS, rows, channels), jnp.float32),
            pltpu.SemaphoreType.DMA((2, channels // min(256, channels))),
        ],
        compiler_params=pltpu.CompilerParams(vmem_limit_bytes=VMEM_LIMIT - 4 * before.size),
        name="last_stacks",
    )(source, rotation_tables(length, length // 2), receiver, before)


def on_device(record, valid, sources):
    wide_count = lax.axis_size("wide")
    rep_count = lax.axis_size("rep")
    length = record.shape[1]
    picked = pick_sources(record[0], valid, sources)
    before, receiver, source = gather_stacks(record[0], valid, picked, wide_count, rep_count)
    scale = 1.0 / math.sqrt(wide_count * rep_count * (length // 2)) / RAISE
    before, receiver, source = (pltpu.with_memory_space_constraint(kept, pltpu.VMEM) for kept in (before, receiver, source))
    return last_stacks(source, receiver, before, scale, rep_count)


def solution(mesh):
    return jax.shard_map(
        on_device,
        mesh=mesh,
        in_specs=(P(("wide", "rep"), None, None), P(("wide", "rep"), None), P()),
        out_specs=P("rep", None, "wide"),
        check_vma=False,
    )
```
